256 devices in a mesh: qrow: 32 (over z_hi, y, core), kcol: 8 (over z_lo, x).
Axes of the slice: x: 4, y: 4, z: 8 (z_hi: 4, z_lo: 2; z = z_hi * 2 + z_lo), core: 2. Of those that a mesh axis runs over, the one named last changes fastest.
Arguments:
- queries: bfloat16 [32768, 256], P(('qrow', 'kcol'))
- keys: bfloat16 [32768, 128], P(('qrow', 'kcol'))
- values: bfloat16 [32768, 128], P(('qrow', 'kcol'))
- out_grad: bfloat16 [32768, 256], P(('qrow', 'kcol'))
- outputs: bfloat16 [32768, 256], P(('qrow', 'kcol')), as said below
- log_norm: float32 [2, 32768], P(None, ('qrow', 'kcol')), as said below
- perm_blocks: int32 [256], replicated, may hold values from 0 to 255, as said below
- doc_bounds: int32 [16], replicated, may hold values from 0 to 32767, as said below
- block_map: int32 [256, 256], replicated, may hold values from 0 to 1, as said below
Outputs:
- grad_query: float32 [32768, 256], P(('qrow', 'kcol'))
- grad_key: float32 [32768, 128], P(('qrow', 'kcol'))
- grad_value: float32 [32768, 128], P(('qrow', 'kcol'))
The draws below stay inside these ranges and needn't reach their ends.
Inputs may be any that keep to these rules, and one draw needn't show every extreme that they name: `perm_blocks`: every sequence block appears once. `doc_bounds`: strictly increasing, the first entry 0. `block_map`: an entry is 1 exactly where some token of the first block may attend some token of the second under the causal document mask, else 0. `log_norm`: for each head and query, the log of the sum of exp(scores) over the keys it is allowed, with the given queries and keys. `outputs`: the forward attention output of the given queries, keys and values under the same mask, rounded to bfloat16.
All inputs are finite; a program needn't handle non-finite values.
Results may differ from the reference program's by a relative error of at most 0.0029.
Values may be sent and summed in bfloat16 or wider, within the bound.
No kernel may reach another device: no remote copies, remote signals or barrier semaphores. Data moves between devices by JAX's collectives and lax.ppermute only.
A program may use at most 128 MiB of HBM per device.

```python
import math
import jax
import jax.numpy as jnp
from jax import lax

TOK_DEV = 128
HEAD_DIM = 128
HEADS = 2
DOCS = 16
BLOCKS = 256
SEQ = 32768


def shared_integers(key):
    perm_blocks = jax.random.permutation(jax.random.fold_in(key, 101), BLOCKS).astype(jnp.int32)
    cut_points = jax.random.permutation(jax.random.fold_in(key, 102), SEQ - 2)[:DOCS - 2].astype(jnp.int32) + 1
    last_cut = jnp.full((1,), SEQ - 1, jnp.int32)
    doc_bounds = jnp.concatenate([jnp.zeros((1,), jnp.int32), jnp.sort(cut_points), last_cut])
    return (perm_blocks, doc_bounds)


def rough_rows(key, row_count, col_count):
    normal_part = jnp.clip(jax.random.normal(jax.random.fold_in(key, 1), (row_count, col_count), jnp.float32), -6.0, 6.0)
    return normal_part


def shared_floats(key):
    query_rows = rough_rows(jax.random.fold_in(key, 201), SEQ, HEADS * HEAD_DIM).astype(jnp.bfloat16)
    key_rows = rough_rows(jax.random.fold_in(key, 202), SEQ, HEAD_DIM).astype(jnp.bfloat16)
    value_rows = rough_rows(jax.random.fold_in(key, 203), SEQ, HEAD_DIM).astype(jnp.bfloat16)
    grad_rows = rough_rows(jax.random.fold_in(key, 204), SEQ, HEADS * HEAD_DIM).astype(jnp.bfloat16)
    return (query_rows, key_rows, value_rows, grad_rows)


def starts_from(doc_bounds, positions):
    found = jnp.where(doc_bounds[None, :] <= positions[:, None], doc_bounds[None, :], 0)
    return jnp.max(found, axis=1).astype(jnp.int32)


def device_order(perm_blocks):
    row_ids = jnp.arange(SEQ, dtype=jnp.int32)
    return (perm_blocks[row_ids // TOK_DEV] * TOK_DEV + row_ids % TOK_DEV).astype(jnp.int32)


def forward_pass(key):
    perm_blocks, doc_bounds = shared_integers(key)
    query_rows, key_rows, value_rows, grad_rows = shared_floats(key)
    score_scale = HEAD_DIM ** (-0.5)
    highest = lax.Precision.HIGHEST
    seq_ids = jnp.arange(SEQ, dtype=jnp.int32)
    starts = starts_from(doc_bounds, seq_ids)
    block_rows = math.gcd(SEQ, 512)
    norm_parts = []
    output_parts = []
    for begin_row in range(0, SEQ, block_rows):
        end_row = begin_row + block_rows
        query_part = query_rows[begin_row:end_row].astype(jnp.float32).reshape(block_rows, HEADS, HEAD_DIM)
        scores = jnp.einsum('qhd,kd->hqk', query_part, key_rows[:end_row].astype(jnp.float32), precision=highest) * score_scale
        allowed = (starts[begin_row:end_row, None] <= seq_ids[None, :end_row]) & (seq_ids[None, :end_row] <= seq_ids[begin_row:end_row, None])
        masked = jnp.where(allowed[None], scores, -jnp.inf)
        log_total = jax.nn.logsumexp(masked, axis=2)
        weights = jnp.exp(masked - log_total[:, :, None])
        mixed = jnp.einsum('hqk,kd->qhd', weights, value_rows[:end_row].astype(jnp.float32), precision=highest)
        norm_parts.append(log_total)
        output_parts.append(mixed.reshape(block_rows, HEADS * HEAD_DIM))
    log_norm = jnp.concatenate(norm_parts, axis=1)
    outputs = jnp.concatenate(output_parts, axis=0).astype(jnp.bfloat16)
    return (log_norm, outputs, perm_blocks)


def draw_queries(key, part):
    perm_blocks = shared_integers(key)[0]
    return shared_floats(key)[0][device_order(perm_blocks)]


def draw_keys(key, part):
    perm_blocks = shared_integers(key)[0]
    return shared_floats(key)[1][device_order(perm_blocks)]


def draw_values(key, part):
    perm_blocks = shared_integers(key)[0]
    return shared_floats(key)[2][device_order(perm_blocks)]


def draw_out_grad(key, part):
    perm_blocks = shared_integers(key)[0]
    return shared_floats(key)[3][device_order(perm_blocks)]


def draw_outputs(key, part):
    log_norm, outputs, perm_blocks = forward_pass(key)
    return outputs[device_order(perm_blocks)]


def draw_log_norm(key, part):
    log_norm, outputs, perm_blocks = forward_pass(key)
    return log_norm[:, device_order(perm_blocks)]


def draw_perm_blocks(key, part):
    return shared_integers(key)[0]


def draw_doc_bounds(key, part):
    return shared_integers(key)[1]


def draw_block_map(key, part):
    doc_bounds = shared_integers(key)[1]
    block_ids = jnp.arange(BLOCKS, dtype=jnp.int32)
    first_starts = starts_from(doc_bounds, block_ids * TOK_DEV)
    earlier = block_ids[None, :] <= block_ids[:, None]
    reached = first_starts[:, None] <= block_ids[None, :] * TOK_DEV + TOK_DEV - 1
    return (earlier & reached).astype(jnp.int32)


def setup_inputs(seed: int = 0) -> dict:
    key_list = jax.random.split(jax.random.key(seed), 10)
    return {
        "queries": draw_queries(jax.random.fold_in(key_list[9], 71), 0),
        "keys": draw_keys(jax.random.fold_in(key_list[9], 71), 0),
        "values": draw_values(jax.random.fold_in(key_list[9], 71), 0),
        "out_grad": draw_out_grad(jax.random.fold_in(key_list[9], 71), 0),
        "outputs": draw_outputs(jax.random.fold_in(key_list[9], 71), 0),
        "log_norm": draw_log_norm(jax.random.fold_in(key_list[9], 71), 0),
        "perm_blocks": draw_perm_blocks(jax.random.fold_in(key_list[9], 71), 0),
        "doc_bounds": draw_doc_bounds(jax.random.fold_in(key_list[9], 71), 0),
        "block_map": draw_block_map(jax.random.fold_in(key_list[9], 71), 0),
    }


def doc_starts(doc_bounds, positions):
    found = jnp.where(doc_bounds[None, :] <= positions[:, None], doc_bounds[None, :], 0)
    return jnp.max(found, axis=1).astype(jnp.int32)


def reference(queries, keys, values, out_grad, outputs, log_norm, perm_blocks, doc_bounds, block_map):
    score_scale = HEAD_DIM ** -0.5
    highest = lax.Precision.HIGHEST
    row_ids = jnp.arange(SEQ, dtype=jnp.int32)
    positions = (perm_blocks[row_ids // TOK_DEV] * TOK_DEV + row_ids % TOK_DEV).astype(jnp.int32)
    seq_order = jnp.argsort(positions).astype(jnp.int32)
    query_rows = queries[seq_order].astype(jnp.float32).reshape(SEQ, HEADS, HEAD_DIM)
    cotangent = out_grad[seq_order].astype(jnp.float32).reshape(SEQ, HEADS, HEAD_DIM)
    key_rows = keys[seq_order].astype(jnp.float32)
    value_rows = values[seq_order].astype(jnp.float32)
    products = (out_grad.astype(jnp.float32) * outputs.astype(jnp.float32)).reshape(SEQ, HEADS, HEAD_DIM)
    row_delta = jnp.sum(products, axis=2)[seq_order].T
    norm_rows = log_norm[:, seq_order]
    starts = doc_starts(doc_bounds, row_ids)
    block_ids = (row_ids // TOK_DEV).astype(jnp.int32)
    block_rows = math.gcd(SEQ, 512)
    grad_key = jnp.zeros((SEQ, HEAD_DIM), jnp.float32)
    grad_value = jnp.zeros((SEQ, HEAD_DIM), jnp.float32)
    query_parts = []
    for begin_row in range(0, SEQ, block_rows):
        end_row = begin_row + block_rows
        query_part = query_rows[begin_row:end_row]
        grad_part = cotangent[begin_row:end_row]
        tile_table = block_map[block_ids[begin_row:end_row]][:, block_ids[:end_row]]
        allowed = (starts[begin_row:end_row, None] <= row_ids[None, :end_row]) & (row_ids[None, :end_row] <= row_ids[begin_row:end_row, None]) & (tile_table == 1)
        scores = jnp.einsum("qhd,kd->hqk", query_part, key_rows[:end_row], precision=highest) * score_scale
        weights = jnp.where(allowed[None], jnp.exp(scores - norm_rows[:, begin_row:end_row, None]), 0.0)
        weights_b = weights.astype(jnp.bfloat16).astype(jnp.float32)
        grad_value = grad_value.at[:end_row].add(jnp.einsum("hqk,qhd->kd", weights_b, grad_part, precision=highest))
        dprob = jnp.einsum("qhd,kd->hqk", grad_part, value_rows[:end_row], precision=highest)
        dscore = (weights * (dprob - row_delta[:, begin_row:end_row, None]) * score_scale).astype(jnp.bfloat16).astype(jnp.float32)
        query_parts.append(jnp.einsum("hqk,kd->qhd", dscore, key_rows[:end_row], precision=highest).reshape(block_rows, HEADS * HEAD_DIM))
        grad_key = grad_key.at[:end_row].add(jnp.einsum("hqk,qhd->kd", dscore, query_part, precision=highest))
    grad_query = jnp.concatenate(query_parts, axis=0)
    return grad_query[positions], grad_key[positions], grad_value[positions]
```

```python
import jax
import jax.numpy as jnp
import numpy as np
from jax import lax
from jax.experimental import pallas as pl
from jax.experimental.pallas import tpu as pltpu
from jax.sharding import PartitionSpec as P

AXES = ("qrow", "kcol")
LOG2E = 1.4426950408889634
TOK = 128
AUX = 16
QROWS = 4 * TOK + AUX
GROUP = 16


def coords(i):
    return (i // 64) * 2 + (i // 4) % 2, (i // 16) % 4, (i // 8) % 2, i % 4


def index(z, y, core, x):
    return (((z // 2) * 4 + y) * 2 + core) * 8 + (z % 2) * 4 + x


def pair4(i, flip):
    return 3 - i if flip else i ^ 1


def pair_z(z, y, c, x):
    return (z ^ 1 if c == 0 else (z + (1 if z % 2 else -1)) % 8), y, c, x


def pair_x1(z, y, c, x):
    return z, y, c, pair4(x, c == 1)


def pair_x2(z, y, c, x):
    return z, y, c, pair4(x, c == 0)


def pair_core(z, y, c, x):
    return z, y, 1 - c, x


def pair_z1(z, y, c, x):
    return 2 * pair4(z // 2, c == 1) + z % 2, y, c, x


def pair_z2(z, y, c, x):
    return 2 * pair4(z // 2, c == 0) + z % 2, y, c, x


def pair_y1(z, y, c, x):
    return z, pair4(y, c == 1), c, x


def pair_y2(z, y, c, x):
    return z, pair4(y, c == 0), c, x


def partners(pair):
    return np.array([index(*pair(*coords(i))) for i in range(256)])


def slot_table(pairs):
    table = np.arange(256)[:, None]
    for pair in pairs:
        table = np.concatenate([table, table[partners(pair)]], axis=1)
    return table


def swap(value, pair):
    to = partners(pair)
    return lax.ppermute(value, AXES, [(i, int(to[i])) for i in range(256)])


def prep_kernel(q_ref, g_ref, o_ref, n_ref, k_ref, v_ref, qpay_ref, kvpay_ref):
    rows = [n_ref[0:1, :], n_ref[1:2, :]]
    for head in range(2):
        cols = slice(head * TOK, (head + 1) * TOK)
        qpay_ref[head * TOK : (head + 1) * TOK, :] = q_ref[:, cols]
        qpay_ref[(2 + head) * TOK : (3 + head) * TOK, :] = g_ref[:, cols]
        product = g_ref[:, cols].astype(jnp.float32) * o_ref[:, cols].astype(jnp.float32)
        rows.append(jnp.sum(product.T, axis=0, keepdims=True))
    exact = jnp.concatenate(rows, axis=0)
    high = exact.astype(jnp.bfloat16).astype(jnp.float32)
    rest = exact - high
    mid = rest.astype(jnp.bfloat16).astype(jnp.float32)
    low = rest - mid
    parts = jnp.concatenate([high, mid, low, jnp.zeros_like(low)], axis=0)
    qpay_ref[4 * TOK :, :] = parts.astype(jnp.bfloat16)
    kvpay_ref[0:TOK, :] = k_ref[...]
    kvpay_ref[TOK:, :] = v_ref[...]


def list_kernel(perm_ref, bounds_ref, ids_ref, list_ref, base_ref, rows_ref):
    lane = lax.broadcasted_iota(jnp.int32, (1, TOK), 1)
    for slot in range(GROUP):
        base_ref[slot] = perm_ref[ids_ref[GROUP + slot]] * TOK
        first = perm_ref[ids_ref[slot]] * TOK
        position = first + lane
        start = jnp.zeros((1, TOK), jnp.int32)
        first_start = jnp.int32(0)
        for doc in range(16):
            bound = bounds_ref[doc]
            start = jnp.where(position >= bound, bound, start)
            first_start = jnp.where(first >= bound, bound, first_start)
        base_ref[GROUP + 1 + slot] = first
        base_ref[2 * GROUP + 1 + slot] = first_start
        rows_ref[slot, 0:1, :] = start
        rows_ref[slot, 1:2, :] = position
    base_ref[GROUP] = jnp.int32(-(1 << 20))

    def outer(ks, count):
        key_base = base_ref[ks]

        def inner(qs, count):
            active = (key_base <= base_ref[GROUP + 1 + qs]) & (
                base_ref[2 * GROUP + 1 + qs] <= key_base + (TOK - 1)
            )
            list_ref[1 + count] = qs + GROUP * ks
            return count + active.astype(jnp.int32)

        return lax.fori_loop(0, GROUP, inner, count, unroll=True)

    count = lax.fori_loop(0, GROUP, outer, jnp.int32(0))
    list_ref[0] = count
    list_ref[1 + count] = jnp.int32(GROUP * GROUP)


NT = (((1,), (1,)), ((), ()))


def main_kernel(list_ref, base_ref, rows_ref, qa_ref, qb_ref, kv_ref, dqa_ref, dqb_ref, ga_ref, gb_ref, dq, dkv, aux, kt):
    half = GROUP // 2
    scale = TOK ** (-0.5)
    dq[...] = jnp.zeros_like(dq)
    dkv[...] = jnp.zeros_like(dkv)
    for slot in range(GROUP):
        q_ref = qa_ref if slot < half else qb_ref
        parts = q_ref[slot % half, 4 * TOK :, :].astype(jnp.float32)
        exact = (parts[8:12] + parts[4:8]) + parts[0:4]
        for head in range(2):
            cols = slice(head * TOK, (head + 1) * TOK)
            aux[slot, 0:1, cols] = exact[head : head + 1] * LOG2E
            aux[slot, 1:2, cols] = exact[2 + head : 3 + head]
        kt[slot] = kv_ref[slot, 0:TOK, :].T
    sub = lax.broadcasted_iota(jnp.int32, (TOK, TOK), 0)

    def tile(q_ref, qs, ql, ks):
        kl = ks & (GROUP - 1)
        base = base_ref[ks]
        q = q_ref[ql, 0 : 2 * TOK, :]
        g = q_ref[ql, 2 * TOK : 4 * TOK, :]
        k = kv_ref[kl, 0:TOK, :]
        v = kv_ref[kl, TOK:, :]
        scores = lax.dot_general(k, q, NT, preferred_element_type=jnp.float32)
        dprob = lax.dot_general(v, g, NT, preferred_element_type=jnp.float32)
        allowed = (sub >= rows_ref[qs, 0:1, :] - base) & (sub <= rows_ref[qs, 1:2, :] - base)
        allowed = jnp.concatenate([allowed, allowed], axis=1)
        weights = jnp.where(allowed, jnp.exp2(scores * (scale * LOG2E) - aux[qs, 0:1, :]), 0.0)
        dscore = (weights * (dprob - aux[qs, 1:2, :]) * scale).astype(jnp.bfloat16)
        weights_b = weights.astype(jnp.bfloat16)
        dv = jnp.dot(weights_b, g, preferred_element_type=jnp.float32)
        dk = jnp.dot(dscore, q, preferred_element_type=jnp.float32)
        dqt = jnp.dot(kt[kl], dscore, preferred_element_type=jnp.float32)
        return kl, dv, dk, dqt

    def step(i, carry):
        entry = list_ref[1 + i]
        qs, ks = entry & (GROUP - 1), entry >> 4

        def run(q_ref, ql):
            kl, dv, dk, dqt = tile(q_ref, qs, ql, ks)
            dkv[kl, 0:TOK, :] += dk
            dkv[kl, TOK:, :] += dv
            dq[qs] += dqt

        pl.when(qs < half)(lambda: run(qa_ref, qs))
        pl.when(qs >= half)(lambda: run(qb_ref, qs - half))
        return carry

    lax.fori_loop(0, list_ref[0], step, 0)
    dqa_ref[...] = dq[0:half]
    dqb_ref[...] = dq[half:]
    ga_ref[...] = dkv[0:half]
    gb_ref[...] = dkv[half:].astype(jnp.bfloat16)


def spec(space=pltpu.VMEM):
    return pl.BlockSpec(memory_space=space)


def body(queries, keys, values, out_grad, outputs, log_norm, perm_blocks, doc_bounds, block_map):
    del block_map
    half = GROUP // 2
    me = lax.axis_index("qrow") * lax.axis_size("kcol") + lax.axis_index("kcol")
    ids = jnp.asarray(
        np.concatenate(
            [slot_table([pair_z, pair_x1, pair_x2, pair_core]), slot_table([pair_z1, pair_z2, pair_y1, pair_y2])], axis=1
        ).astype(np.int32)
    )[me]
    params = pltpu.CompilerParams(vmem_limit_bytes=48 * 1024 * 1024)
    q1, kv1 = pl.pallas_call(
        prep_kernel,
        out_shape=(
            jax.ShapeDtypeStruct((QROWS, TOK), jnp.bfloat16),
            jax.ShapeDtypeStruct((2 * TOK, TOK), jnp.bfloat16),
        ),
        in_specs=[spec()] * 6,
        out_specs=(spec(), spec()),
        compiler_params=params,
        name="prep",
    )(queries, out_grad, outputs, log_norm, keys, values)
    tiles, bases, rows = pl.pallas_call(
        list_kernel,
        out_shape=(
            jax.ShapeDtypeStruct((GROUP * GROUP + 8,), jnp.int32),
            jax.ShapeDtypeStruct((64,), jnp.int32),
            jax.ShapeDtypeStruct((GROUP, 8, TOK), jnp.int32),
        ),
        in_specs=[spec(pltpu.SMEM)] * 3,
        out_specs=(spec(pltpu.SMEM), spec(pltpu.SMEM), spec()),
        compiler_params=params,
        name="tiles",
    )(perm_blocks, doc_bounds, ids)

    q2 = jnp.concatenate([q1[None], swap(q1, pair_z)[None]])
    kv2 = jnp.concatenate([kv1[None], swap(kv1, pair_z1)[None]])
    q4 = jnp.concatenate([q2, swap(q2, pair_x1)])
    kv4 = jnp.concatenate([kv2, swap(kv2, pair_z2)])
    q8 = jnp.concatenate([q4, swap(q4, pair_x2)])
    kv8 = jnp.concatenate([kv4, swap(kv4, pair_y1)])
    other8 = swap(q8, pair_core)
    kv16 = jnp.concatenate([kv8, swap(kv8, pair_y2)])

    dqa, dqb, ga, gb = pl.pallas_call(
        main_kernel,
        out_shape=(
            jax.ShapeDtypeStruct((half, TOK, 2 * TOK), jnp.float32),
            jax.ShapeDtypeStruct((half, TOK, 2 * TOK), jnp.float32),
            jax.ShapeDtypeStruct((half, 2 * TOK, TOK), jnp.float32),
            jax.ShapeDtypeStruct((half, 2 * TOK, TOK), jnp.bfloat16),
        ),
        in_specs=[spec(pltpu.SMEM)] * 2 + [spec()] * 4,
        out_specs=(spec(),) * 4,
        scratch_shapes=[
            pltpu.VMEM((GROUP, TOK, 2 * TOK), jnp.float32),
            pltpu.VMEM((GROUP, 2 * TOK, TOK), jnp.float32),
            pltpu.VMEM((GROUP, 8, 2 * TOK), jnp.float32),
            pltpu.VMEM((GROUP, TOK, TOK), jnp.bfloat16),
        ],
        compiler_params=params,
        cost_estimate=pl.CostEstimate(flops=10**9, bytes_accessed=10**7, transcendentals=10**6),
        name="main",
    )(tiles, bases, rows, q8, other8, kv16)

    dq8 = dqa + swap(dqb, pair_core)
    g8 = ga + swap(gb, pair_y2).astype(jnp.float32)
    dq4 = dq8[:4] + swap(dq8[4:].astype(jnp.bfloat16), pair_x2).astype(jnp.float32)
    g4 = g8[:4] + swap(g8[4:].astype(jnp.bfloat16), pair_y1).astype(jnp.float32)
    dq2 = dq4[:2] + swap(dq4[2:].astype(jnp.bfloat16), pair_x1).astype(jnp.float32)
    g2 = g4[:2] + swap(g4[2:], pair_z2)
    dq1 = dq2[0] + swap(dq2[1], pair_z)
    g1 = g2[0] + swap(g2[1], pair_z1)
    grad_query = dq1.reshape(TOK, 2, TOK).transpose(2, 1, 0).reshape(TOK, 2 * TOK)
    return grad_query, g1[:TOK], g1[TOK:]


def solution(mesh):
    rows, cols = P(AXES, None), P(None, AXES)
    return jax.shard_map(
        body,
        mesh=mesh,
        in_specs=(rows, rows, rows, rows, rows, cols, P(), P(), P()),
        out_specs=(rows, rows, rows),
        check_vma=False,
    )
```

```python
import jax
import jax.numpy as jnp
import numpy as np
from jax import lax
from jax.experimental import pallas as pl
from jax.experimental.pallas import tpu as pltpu
from jax.sharding import PartitionSpec as P

AXES = ("qrow", "kcol")
LOG2E = 1.4426950408889634
TOK = 128
AUX = 16
QROWS = 4 * TOK + AUX
GROUP = 16
HALF = GROUP // 2
PARTS = ((0, 8), (12, 16), (8, 12))
LISTS, LIST = 8, GROUP * HALF + 8
UNROLL = (4, 2, 2)


def coords(i):
    return (i // 64) * 2 + (i // 4) % 2, (i // 16) % 4, (i // 8) % 2, i % 4


def index(z, y, core, x):
    return (((z // 2) * 4 + y) * 2 + core) * 8 + (z % 2) * 4 + x


def pair4(i, flip):
    return 3 - i if flip else i ^ 1


def pair_z(z, y, c, x):
    return 2 * pair4(z // 2, False) + z % 2, y, c, x


def pair_core(z, y, c, x):
    return z, y, 1 - c, x


def pair_z1(z, y, c, x):
    return 2 * pair4(z // 2, True) + z % 2, y, c, x


def pair_z2(z, y, c, x):
    return z ^ 1, y, c, x


def pair_x1(z, y, c, x):
    return z, y, c, pair4(x, c == 1)


def pair_x2(z, y, c, x):
    return z, y, c, pair4(x, c == 0)


def pair_z3(z, y, c, x):
    return pair_z1(*pair_z2(z, y, c, x))


def pair_y1(z, y, c, x):
    return z, pair4(y, c == 1), c, x


def pair_y2(z, y, c, x):
    return z, pair4(y, c == 0), c, x


def partners(pair):
    return np.array([index(*pair(*coords(i))) for i in range(256)])


def joined(pairs):
    table = np.arange(256)[:, None]
    for pair in pairs:
        table = np.concatenate([table, table[partners(pair)]], axis=1)
    return table


def swap(value, pair):
    to = partners(pair)
    return lax.ppermute(value, AXES, [(i, int(to[i])) for i in range(256)])


def slot_tables():
    queries = joined([pair_z, pair_x1, pair_x2, pair_core])
    keys = joined([pair_z1, pair_z2, pair_y1, pair_y2])
    return np.concatenate([queries, keys], axis=1).astype(np.int32)


def prep_kernel(q_ref, g_ref, o_ref, n_ref, k_ref, v_ref, qpay_ref, kvpay_ref):
    rows = [n_ref[0:1, :], n_ref[1:2, :]]
    for head in range(2):
        cols = slice(head * TOK, (head + 1) * TOK)
        qpay_ref[0, head * TOK : (head + 1) * TOK, :] = q_ref[:, cols]
        qpay_ref[0, (2 + head) * TOK : (3 + head) * TOK, :] = g_ref[:, cols]
        product = g_ref[:, cols].astype(jnp.float32) * o_ref[:, cols].astype(jnp.float32)
        rows.append(jnp.sum(product.T, axis=0, keepdims=True))
    exact = jnp.concatenate(rows, axis=0)
    high = exact.astype(jnp.bfloat16).astype(jnp.float32)
    rest = exact - high
    mid = rest.astype(jnp.bfloat16).astype(jnp.float32)
    low = rest - mid
    parts = jnp.concatenate([high, mid, low, jnp.zeros_like(low)], axis=0)
    qpay_ref[0, 4 * TOK :, :] = parts.astype(jnp.bfloat16)
    kvpay_ref[0, 0:TOK, :] = k_ref[...]
    kvpay_ref[0, TOK:, :] = v_ref[...]


def list_kernel(perm_ref, bounds_ref, ids_ref, list_ref, base_ref, rows_ref):
    lane = lax.broadcasted_iota(jnp.int32, (1, TOK), 1)
    for slot in range(GROUP):
        base_ref[slot] = perm_ref[ids_ref[GROUP + slot]] * TOK
        first = perm_ref[ids_ref[slot]] * TOK
        position = first + lane
        start = jnp.zeros((1, TOK), jnp.int32)
        first_start = jnp.int32(0)
        for doc in range(16):
            bound = bounds_ref[doc]
            start = jnp.where(position >= bound, bound, start)
            first_start = jnp.where(first >= bound, bound, first_start)
        base_ref[GROUP + 1 + slot] = first
        base_ref[2 * GROUP + 1 + slot] = first_start
        rows_ref[slot, 0:1, :] = start
        rows_ref[slot, 1:2, :] = position
    base_ref[GROUP] = jnp.int32(-(1 << 20))

    def outer(ks, count, place):
        key_base = base_ref[ks]

        def inner(qs, count):
            active = (key_base <= base_ref[GROUP + 1 + qs]) & (
                base_ref[2 * GROUP + 1 + qs] <= key_base + (TOK - 1)
            )
            list_ref[place + count] = qs + GROUP * ks
            return count + active.astype(jnp.int32)

        return lax.fori_loop(0, GROUP, inner, count, unroll=True)

    for part, (begin, end) in enumerate(PARTS):
        place = LISTS + part * LIST
        count = lax.fori_loop(begin, end, lambda ks, count: outer(ks, count, place), jnp.int32(0))
        list_ref[part] = count
        for extra in range(UNROLL[part] - 1):
            list_ref[place + count + extra] = jnp.int32(GROUP * GROUP)


def join_kernel(a0, a1, b0, b1, a_ref, b_ref):
    for first, second, ref in ((a0, a1, a_ref), (b0, b1, b_ref)):
        split = first.shape[0]
        ref[0:split] = first[...]
        ref[split:] = second[...]


def hold_kernel(a0, b0, a_ref, b_ref):
    a_ref[...] = a0[...]
    b_ref[...] = b0[...]


def finish_kernel(g_ref, g1, g2, g3, dq_ref, dq_in, query_ref, key_ref, value_ref):
    for ref, rows in ((key_ref, slice(0, TOK)), (value_ref, slice(TOK, 2 * TOK))):
        total = g_ref[0, rows, :]
        for part in (g1, g2, g3):
            total = total + part[0, rows, :].astype(jnp.float32)
        ref[...] = total
    for head in range(2):
        cols = slice(head * TOK, (head + 1) * TOK)
        query_ref[:, cols] = (dq_ref[0, :, cols] + dq_in[0, :, cols].astype(jnp.float32)).T


NT = (((1,), (1,)), ((), ()))


def walk(part, list_ref, base_ref, rows_ref, q_all, aux, kv_refs, kv_all, kt, dq, dkv):
    scale = TOK ** (-0.5)
    begin = PARTS[part][0]
    unroll = UNROLL[part]
    place = LISTS + part * LIST
    sub = lax.broadcasted_iota(jnp.int32, (TOK, TOK), 0)
    for slot in range(PARTS[part][1] - begin):
        block = kv_refs[slot // 4][slot % 4]
        kv_all[slot] = block
        kt[slot] = block[0:TOK, :].T
    dkv[...] = jnp.zeros_like(dkv)

    def tile(entry):
        qs, ks = entry & (GROUP - 1), entry >> 4
        base = base_ref[ks]
        kl = jnp.where(ks == GROUP, 0, ks - begin)
        q = q_all[qs, 0 : 2 * TOK, :]
        g = q_all[qs, 2 * TOK : 4 * TOK, :]
        k = kv_all[kl, 0:TOK, :]
        v = kv_all[kl, TOK:, :]
        scores = lax.dot_general(k, q, NT, preferred_element_type=jnp.float32)
        dprob = lax.dot_general(v, g, NT, preferred_element_type=jnp.float32)
        allowed = (sub >= rows_ref[qs, 0:1, :] - base) & (sub <= rows_ref[qs, 1:2, :] - base)
        allowed = jnp.concatenate([allowed, allowed], axis=1)
        weights = jnp.where(allowed, jnp.exp2(scores * (scale * LOG2E) - aux[qs, 0:1, :]), 0.0)
        dscore = (weights * (dprob - aux[qs, 1:2, :]) * scale).astype(jnp.bfloat16)
        dv = jnp.dot(weights.astype(jnp.bfloat16), g, preferred_element_type=jnp.float32)
        dk = jnp.dot(dscore, q, preferred_element_type=jnp.float32)
        dqt = jnp.dot(kt[kl], dscore, preferred_element_type=jnp.float32)
        return qs, kl, dqt, dk, dv

    def step(i, carry):
        done = [tile(list_ref[place + unroll * i + j]) for j in range(unroll)]
        for qs, kl, dqt, dk, dv in done:
            dkv[kl, TOK:, :] += dv
            dkv[kl, 0:TOK, :] += dk
            dq[qs] += dqt
        return carry

    lax.fori_loop(0, (list_ref[part] + (unroll - 1)) // unroll, step, 0)


def first_kernel(list_ref, base_ref, rows_ref, q0, q1, q2, q3, kv0, kv1, q_all, aux, dq, dkv, kv_all, kt):
    for part, q_ref in enumerate((q0, q1, q2, q3)):
        q_all[4 * part : 4 * part + 4] = q_ref[...]
        for slot in range(4):
            parts = q_ref[slot, 4 * TOK :, :].astype(jnp.float32)
            exact = (parts[8:12] + parts[4:8]) + parts[0:4]
            for head in range(2):
                cols = slice(head * TOK, (head + 1) * TOK)
                aux[4 * part + slot, 0:1, cols] = exact[head : head + 1] * LOG2E
                aux[4 * part + slot, 1:2, cols] = exact[2 + head : 3 + head]
    dq[...] = jnp.zeros_like(dq)
    walk(0, list_ref, base_ref, rows_ref, q_all, aux, (kv0, kv1), kv_all, kt, dq, dkv)


def far_kernel(list_ref, base_ref, rows_ref, q_all, aux, before, kv_ref, dq, out_ref, dkv, kv_all, kt):
    dq[...] = before[...]
    walk(1, list_ref, base_ref, rows_ref, q_all, aux, (kv_ref,), kv_all, kt, dq, dkv)
    out_ref[...] = dkv[...].astype(jnp.bfloat16)


def last_kernel(list_ref, base_ref, rows_ref, q_all, aux, before, kv_ref, dqa_ref, *refs):
    outs, (out_ref, dq, dkv, kv_all, kt) = refs[:4], refs[4:]
    dq[...] = before[...]
    walk(2, list_ref, base_ref, rows_ref, q_all, aux, (kv_ref,), kv_all, kt, dq, dkv)
    dqa_ref[...] = dq[0:HALF]
    for i, ref in enumerate(outs):
        ref[...] = dq[HALF + 2 * i : HALF + 2 * i + 2].astype(jnp.bfloat16)
    out_ref[...] = dkv[...].astype(jnp.bfloat16)


def spec(space=pltpu.VMEM):
    return pl.BlockSpec(memory_space=space)


def together(*arrays):
    return lax.optimization_barrier(arrays)


def whole(array):
    return pl.BlockSpec(array.shape, lambda i: (0, 0))


def body(queries, keys, values, out_grad, outputs, log_norm, perm_blocks, doc_bounds, block_map):
    del block_map
    me = lax.axis_index("qrow") * lax.axis_size("kcol") + lax.axis_index("kcol")
    ids = jnp.asarray(slot_tables())[me]
    params = pltpu.CompilerParams(vmem_limit_bytes=40 * 1024 * 1024)
    q1, kv1 = pl.pallas_call(
        prep_kernel,
        out_shape=(
            jax.ShapeDtypeStruct((1, QROWS, TOK), jnp.bfloat16),
            jax.ShapeDtypeStruct((1, 2 * TOK, TOK), jnp.bfloat16),
        ),
        grid=(1,),
        in_specs=[whole(a) for a in (queries, out_grad, outputs, log_norm, keys, values)],
        out_specs=(spec(), spec()),
        compiler_params=pltpu.CompilerParams(vmem_limit_bytes=60 * 1024 * 1024),
        name="prep",
    )(queries, out_grad, outputs, log_norm, keys, values)
    tiles, bases, rows = pl.pallas_call(
        list_kernel,
        out_shape=(
            jax.ShapeDtypeStruct((LISTS + 3 * LIST,), jnp.int32),
            jax.ShapeDtypeStruct((64,), jnp.int32),
            jax.ShapeDtypeStruct((GROUP, 8, TOK), jnp.int32),
        ),
        in_specs=[spec(pltpu.SMEM)] * 3,
        out_specs=(spec(pltpu.SMEM), spec(pltpu.SMEM), spec()),
        compiler_params=params,
        name="tiles",
    )(perm_blocks, doc_bounds, ids)

    narrow, wide = jnp.bfloat16, jnp.float32

    def shape(*dims, dtype=wide):
        return jax.ShapeDtypeStruct(dims, dtype)

    def join(q0, q_in, kv0, kv_in):
        n = 2 * q0.shape[0]
        return pl.pallas_call(
            join_kernel,
            out_shape=(shape(n, *q0.shape[1:], dtype=narrow), shape(n, *kv0.shape[1:], dtype=narrow)),
            in_specs=[spec()] * 4,
            out_specs=(spec(),) * 2,
            compiler_params=params,
            name="join",
        )(q0, q_in, kv0, kv_in)

    def compute(kernel, scalars, arrays, outs, scratch, name):
        return pl.pallas_call(
            kernel,
            out_shape=outs,
            in_specs=[spec(pltpu.SMEM)] * 2 + [spec()] * (1 + len(arrays)),
            out_specs=(spec(),) * len(outs),
            scratch_shapes=scratch,
            compiler_params=params,
            cost_estimate=pl.CostEstimate(flops=3 * 10**9, bytes_accessed=10**7, transcendentals=10**6),
            name=name,
        )(*scalars, *arrays)

    held = pl.pallas_call(
        hold_kernel,
        out_shape=(shape(*q1.shape, dtype=narrow), shape(*kv1.shape, dtype=narrow)),
        in_specs=[spec()] * 2,
        out_specs=(spec(),) * 2,
        compiler_params=params,
        name="hold",
    )(q1, kv1)
    q_in, kv_in, q1, kv1 = together(swap(q1, pair_z), swap(kv1, pair_z1), *held)
    q2, kv2 = join(q1, q_in, kv1, kv_in)
    q_in, kv_in = together(swap(q2, pair_x1), swap(kv2, pair_z2))
    q4, kv4 = join(q2, q_in, kv2, kv_in)
    q_x, kv_y1, kv_y2, q_core, *scalars = together(
        swap(q4, pair_x2), swap(kv4, pair_y1), swap(kv4, pair_y2), swap(q4, pair_core), tiles, bases, rows
    )
    qx_core, kv_far = swap(q_x, pair_core), swap(kv_y1, pair_y2)

    def room(slots):
        return [pltpu.VMEM((slots, 2 * TOK, TOK), narrow), pltpu.VMEM((slots, TOK, TOK), narrow)]

    dq_shape, g_rows = (TOK, 2 * TOK), (2 * TOK, TOK)
    q_all, aux, dq, g = compute(
        first_kernel,
        scalars,
        (q4, q_x, q_core, qx_core, kv4, kv_y1),
        (
            shape(GROUP, QROWS, TOK, dtype=narrow),
            shape(GROUP, 8, 2 * TOK),
            shape(GROUP, *dq_shape),
            shape(HALF, *g_rows),
        ),
        room(8),
        "first",
    )
    dq, far = compute(
        far_kernel,
        scalars,
        (q_all, aux, dq, kv_far),
        (shape(GROUP, *dq_shape), shape(4, *g_rows, dtype=narrow)),
        [pltpu.VMEM((4, *g_rows), wide)] + room(4),
        "far",
    )
    dqa, *others, near = compute(
        last_kernel,
        scalars,
        (q_all, aux, dq, kv_y2),
        (shape(HALF, *dq_shape),) + (shape(2, *dq_shape, dtype=narrow),) * 4 + (shape(4, *g_rows, dtype=narrow),),
        [pltpu.VMEM((GROUP, *dq_shape), wide), pltpu.VMEM((4, *g_rows), wide)] + room(4),
        "last",
    )

    far_in, *others = together(swap(far, pair_y2), *[swap(part, pair_core) for part in others])
    b_in, c_in = jnp.concatenate(others[:2]), jnp.concatenate(others[2:])
    far = g[4:] + far_in.astype(wide)
    near_in, far_in, dq_in = together(
        swap(near, pair_y2), swap(far.astype(narrow), pair_y1), swap((dqa[4:] + c_in.astype(wide)).astype(narrow), pair_x2)
    )
    g, dq = (g[:4] + near_in.astype(wide)) + far_in.astype(wide), (dqa[:4] + b_in.astype(wide)) + dq_in.astype(wide)
    g_in = [swap(g[i : i + 1].astype(narrow), pair) for i, pair in enumerate((pair_z1, pair_z2, pair_z3), 1)]
    dq = dq[:2] + swap(dq[2:].astype(narrow), pair_x1).astype(wide)
    dq_in = swap(dq[1:].astype(narrow), pair_z)
    return pl.pallas_call(
        finish_kernel,
        out_shape=(shape(TOK, 2 * TOK), shape(TOK, TOK), shape(TOK, TOK)),
        in_specs=[spec()] * 6,
        out_specs=(spec(),) * 3,
        compiler_params=params,
        name="finish",
    )(g, *g_in, dq, dq_in)


def solution(mesh):
    rows, cols = P(AXES, None), P(None, AXES)
    return jax.shard_map(
        body,
        mesh=mesh,
        in_specs=(rows, rows, rows, rows, rows, cols, P(), P(), P()),
        out_specs=(rows, rows, rows),
        check_vma=False,
    )
```

```python
import jax
import jax.numpy as jnp
import numpy as np
from jax import lax
from jax.experimental import pallas as pl
from jax.experimental.pallas import tpu as pltpu
from jax.sharding import PartitionSpec as P

AXES = ("qrow", "kcol")
LOG2E = 1.4426950408889634
TOK = 128
AUX = 16
QROWS = 4 * TOK + AUX
GROUP = 16
HALF = GROUP // 2
PARTS = ((0, 8), (12, 16), (8, 12))
LISTS, LIST = 8, GROUP * HALF // 2 + 8
UNROLL = (2, 2, 2)


def coords(i):
    return (i // 64) * 2 + (i // 4) % 2, (i // 16) % 4, (i // 8) % 2, i % 4


def index(z, y, core, x):
    return (((z // 2) * 4 + y) * 2 + core) * 8 + (z % 2) * 4 + x


def pair4(i, flip):
    return 3 - i if flip else i ^ 1


def pair_z(z, y, c, x):
    return 2 * pair4(z // 2, False) + z % 2, y, c, x


def pair_core(z, y, c, x):
    return z, y, 1 - c, x


def pair_z1(z, y, c, x):
    return 2 * pair4(z // 2, True) + z % 2, y, c, x


def pair_z2(z, y, c, x):
    return z ^ 1, y, c, x


def pair_x1(z, y, c, x):
    return z, y, c, pair4(x, c == 1)


def pair_x2(z, y, c, x):
    return z, y, c, pair4(x, c == 0)


def pair_z3(z, y, c, x):
    return pair_z1(*pair_z2(z, y, c, x))


def pair_y1(z, y, c, x):
    return z, pair4(y, c == 1), c, x


def pair_y2(z, y, c, x):
    return z, pair4(y, c == 0), c, x


def partners(pair):
    return np.array([index(*pair(*coords(i))) for i in range(256)])


def joined(pairs):
    table = np.arange(256)[:, None]
    for pair in pairs:
        table = np.concatenate([table, table[partners(pair)]], axis=1)
    return table


def swap(value, pair):
    to = partners(pair)
    return lax.ppermute(value, AXES, [(i, int(to[i])) for i in range(256)])


def slot_tables():
    queries = joined([pair_z, pair_x1, pair_x2, pair_core])
    keys = joined([pair_z1, pair_z2, pair_y1, pair_y2])
    return np.concatenate([queries, keys], axis=1).astype(np.int32)


def prep_kernel(q_ref, g_ref, o_ref, n_ref, k_ref, v_ref, qpay_ref, kvpay_ref):
    rows = [n_ref[0:1, :], n_ref[1:2, :]]
    for head in range(2):
        cols = slice(head * TOK, (head + 1) * TOK)
        qpay_ref[0, head * TOK : (head + 1) * TOK, :] = q_ref[:, cols]
        qpay_ref[0, (2 + head) * TOK : (3 + head) * TOK, :] = g_ref[:, cols]
        product = g_ref[:, cols].astype(jnp.float32) * o_ref[:, cols].astype(jnp.float32)
        rows.append(jnp.sum(product.T, axis=0, keepdims=True))
    exact = jnp.concatenate(rows, axis=0)
    high = exact.astype(jnp.bfloat16).astype(jnp.float32)
    rest = exact - high
    mid = rest.astype(jnp.bfloat16).astype(jnp.float32)
    low = rest - mid
    parts = jnp.concatenate([high, mid, low, jnp.zeros_like(low)], axis=0)
    qpay_ref[0, 4 * TOK :, :] = parts.astype(jnp.bfloat16)
    kvpay_ref[0, 0:TOK, :] = k_ref[...]
    kvpay_ref[0, TOK:, :] = v_ref[...]


def list_kernel(perm_ref, bounds_ref, ids_ref, list_ref, base_ref, rows_ref):
    lane = lax.broadcasted_iota(jnp.int32, (1, TOK), 1)
    for slot in range(GROUP):
        base_ref[slot] = perm_ref[ids_ref[GROUP + slot]] * TOK
        first = perm_ref[ids_ref[slot]] * TOK
        position = first + lane
        start = jnp.zeros((1, TOK), jnp.int32)
        first_start = jnp.int32(0)
        for doc in range(16):
            bound = bounds_ref[doc]
            start = jnp.where(position >= bound, bound, start)
            first_start = jnp.where(first >= bound, bound, first_start)
        base_ref[GROUP + 1 + slot] = first
        base_ref[2 * GROUP + 1 + slot] = first_start
        rows_ref[slot, 0:1, :] = start
        rows_ref[slot, 1:2, :] = position
    base_ref[GROUP] = jnp.int32(-(1 << 20))

    for part, (begin, end) in enumerate(PARTS):
        place = LISTS + part * LIST

        def outer(qs, count):
            first, first_start = base_ref[GROUP + 1 + qs], base_ref[2 * GROUP + 1 + qs]
            held = jnp.int32(GROUP)
            for ks in range(begin, end):
                base = base_ref[ks]
                active = (base <= first) & (first_start <= base + (TOK - 1))
                full = held != GROUP
                entry = qs + 16 * jnp.where(full, held + 32 * ks, ks + 32 * GROUP)
                list_ref[jnp.where(active, place + count, 0)] = entry
                count = count + (active & full).astype(jnp.int32)
                held = jnp.where(active, jnp.where(full, GROUP, ks), held)
            return count + (held != GROUP).astype(jnp.int32)

        count = lax.fori_loop(0, GROUP, outer, jnp.int32(0))
        list_ref[1 + part] = count
        for extra in range(UNROLL[part] - 1):
            list_ref[place + count + extra] = jnp.int32(16 * (GROUP + 32 * GROUP))


def join_kernel(a0, a1, b0, b1, a_ref, b_ref):
    for first, second, ref in ((a0, a1, a_ref), (b0, b1, b_ref)):
        split = first.shape[0]
        ref[0:split] = first[...]
        ref[split:] = second[...]


def hold_kernel(a0, b0, a_ref, b_ref):
    a_ref[...] = a0[...]
    b_ref[...] = b0[...]


def finish_kernel(g_ref, g1, g2, g3, dq_ref, dq_in, query_ref, key_ref, value_ref):
    for ref, rows in ((key_ref, slice(0, TOK)), (value_ref, slice(TOK, 2 * TOK))):
        total = g_ref[0, rows, :]
        for part in (g1, g2, g3):
            total = total + part[0, rows, :].astype(jnp.float32)
        ref[...] = total
    for head in range(2):
        cols = slice(head * TOK, (head + 1) * TOK)
        query_ref[:, cols] = (dq_ref[0, :, cols] + dq_in[0, :, cols].astype(jnp.float32)).T


NT = (((1,), (1,)), ((), ()))


def walk(part, list_ref, base_ref, rows_ref, q_all, aux, kv_refs, kv_all, kt, dq, dkv):
    scale = TOK ** (-0.5)
    begin = PARTS[part][0]
    unroll = UNROLL[part]
    place = LISTS + part * LIST
    sub = lax.broadcasted_iota(jnp.int32, (TOK, TOK), 0)
    for slot in range(PARTS[part][1] - begin):
        block = kv_refs[slot // 4][slot % 4]
        kv_all[slot] = block
        kt[slot] = block[0:TOK, :].T
    dkv[...] = jnp.zeros_like(dkv)

    def tiles(entry):
        qs = entry & (GROUP - 1)
        slots = [(entry >> shift) & 31 for shift in (4, 9)]
        places = [jnp.where(slot == GROUP, 0, slot - begin) for slot in slots]
        bases = [base_ref[slot] for slot in slots]
        q = q_all[qs, 0 : 2 * TOK, :]
        g = q_all[qs, 2 * TOK : 4 * TOK, :]
        k = jnp.concatenate([kv_all[at, 0:TOK, :] for at in places], axis=0)
        v = jnp.concatenate([kv_all[at, TOK:, :] for at in places], axis=0)
        scores = lax.dot_general(k, q, NT, preferred_element_type=jnp.float32)
        dprob = lax.dot_general(v, g, NT, preferred_element_type=jnp.float32)
        start, position = rows_ref[qs, 0:1, :], rows_ref[qs, 1:2, :]
        allowed = [(sub >= start - base) & (sub <= position - base) for base in bases]
        allowed = jnp.concatenate([jnp.concatenate([part, part], axis=1) for part in allowed], axis=0)
        weights = jnp.where(allowed, jnp.exp2(scores * (scale * LOG2E) - aux[qs, 0:1, :]), 0.0)
        dscore = (weights * (dprob - aux[qs, 1:2, :]) * scale).astype(jnp.bfloat16)
        dv = jnp.dot(weights.astype(jnp.bfloat16), g, preferred_element_type=jnp.float32)
        dk = jnp.dot(dscore, q, preferred_element_type=jnp.float32)
        k_t = jnp.concatenate([kt[at] for at in places], axis=1)
        dqt = jnp.dot(k_t, dscore, preferred_element_type=jnp.float32)
        return qs, places, dqt, dk, dv

    def step(i, carry):
        done = [tiles(list_ref[place + unroll * i + j]) for j in range(unroll)]
        for qs, places, dqt, dk, dv in done:
            for at, rows in zip(places, (slice(0, TOK), slice(TOK, 2 * TOK))):
                dkv[at, TOK:, :] += dv[rows]
                dkv[at, 0:TOK, :] += dk[rows]
            dq[qs] += dqt
        return carry

    lax.fori_loop(0, (list_ref[1 + part] + (unroll - 1)) // unroll, step, 0)


def first_kernel(list_ref, base_ref, rows_ref, q0, q1, q2, q3, kv0, kv1, q_all, aux, dq, dkv, kv_all, kt):
    for part, q_ref in enumerate((q0, q1, q2, q3)):
        q_all[4 * part : 4 * part + 4] = q_ref[...]
        for slot in range(4):
            parts = q_ref[slot, 4 * TOK :, :].astype(jnp.float32)
            exact = (parts[8:12] + parts[4:8]) + parts[0:4]
            for head in range(2):
                cols = slice(head * TOK, (head + 1) * TOK)
                aux[4 * part + slot, 0:1, cols] = exact[head : head + 1] * LOG2E
                aux[4 * part + slot, 1:2, cols] = exact[2 + head : 3 + head]
    dq[...] = jnp.zeros_like(dq)
    walk(0, list_ref, base_ref, rows_ref, q_all, aux, (kv0, kv1), kv_all, kt, dq, dkv)


def far_kernel(list_ref, base_ref, rows_ref, q_all, aux, before, kv_ref, dq, out_ref, dkv, kv_all, kt):
    dq[...] = before[...]
    walk(1, list_ref, base_ref, rows_ref, q_all, aux, (kv_ref,), kv_all, kt, dq, dkv)
    out_ref[...] = dkv[...].astype(jnp.bfloat16)


def last_kernel(list_ref, base_ref, rows_ref, q_all, aux, before, kv_ref, dqa_ref, *refs):
    outs, (out_ref, dq, dkv, kv_all, kt) = refs[:4], refs[4:]
    dq[...] = before[...]
    walk(2, list_ref, base_ref, rows_ref, q_all, aux, (kv_ref,), kv_all, kt, dq, dkv)
    dqa_ref[...] = dq[0:HALF]
    for i, ref in enumerate(outs):
        ref[...] = dq[HALF + 2 * i : HALF + 2 * i + 2].astype(jnp.bfloat16)
    out_ref[...] = dkv[...].astype(jnp.bfloat16)


def spec(space=pltpu.VMEM):
    return pl.BlockSpec(memory_space=space)


def together(*arrays):
    return lax.optimization_barrier(arrays)


def whole(array):
    return pl.BlockSpec(array.shape, lambda i: (0, 0))


def body(queries, keys, values, out_grad, outputs, log_norm, perm_blocks, doc_bounds, block_map):
    del block_map
    me = lax.axis_index("qrow") * lax.axis_size("kcol") + lax.axis_index("kcol")
    ids = jnp.asarray(slot_tables())[me]
    params = pltpu.CompilerParams(vmem_limit_bytes=40 * 1024 * 1024)
    q1, kv1 = pl.pallas_call(
        prep_kernel,
        out_shape=(
            jax.ShapeDtypeStruct((1, QROWS, TOK), jnp.bfloat16),
            jax.ShapeDtypeStruct((1, 2 * TOK, TOK), jnp.bfloat16),
        ),
        grid=(1,),
        in_specs=[whole(a) for a in (queries, out_grad, outputs, log_norm, keys, values)],
        out_specs=(spec(), spec()),
        compiler_params=pltpu.CompilerParams(vmem_limit_bytes=60 * 1024 * 1024),
        name="prep",
    )(queries, out_grad, outputs, log_norm, keys, values)
    tiles, bases, rows = pl.pallas_call(
        list_kernel,
        out_shape=(
            jax.ShapeDtypeStruct((LISTS + 3 * LIST,), jnp.int32),
            jax.ShapeDtypeStruct((64,), jnp.int32),
            jax.ShapeDtypeStruct((GROUP, 8, TOK), jnp.int32),
        ),
        in_specs=[spec(pltpu.SMEM)] * 3,
        out_specs=(spec(pltpu.SMEM), spec(pltpu.SMEM), spec()),
        compiler_params=params,
        name="tiles",
    )(perm_blocks, doc_bounds, ids)

    narrow, wide = jnp.bfloat16, jnp.float32

    def shape(*dims, dtype=wide):
        return jax.ShapeDtypeStruct(dims, dtype)

    def join(q0, q_in, kv0, kv_in):
        n = 2 * q0.shape[0]
        return pl.pallas_call(
            join_kernel,
            out_shape=(shape(n, *q0.shape[1:], dtype=narrow), shape(n, *kv0.shape[1:], dtype=narrow)),
            in_specs=[spec()] * 4,
            out_specs=(spec(),) * 2,
            compiler_params=params,
            name="join",
        )(q0, q_in, kv0, kv_in)

    def compute(kernel, scalars, arrays, outs, scratch, name):
        return pl.pallas_call(
            kernel,
            out_shape=outs,
            in_specs=[spec(pltpu.SMEM)] * 2 + [spec()] * (1 + len(arrays)),
            out_specs=(spec(),) * len(outs),
            scratch_shapes=scratch,
            compiler_params=params,
            cost_estimate=pl.CostEstimate(flops=3 * 10**9, bytes_accessed=10**7, transcendentals=10**6),
            name=name,
        )(*scalars, *arrays)

    held = pl.pallas_call(
        hold_kernel,
        out_shape=(shape(*q1.shape, dtype=narrow), shape(*kv1.shape, dtype=narrow)),
        in_specs=[spec()] * 2,
        out_specs=(spec(),) * 2,
        compiler_params=params,
        name="hold",
    )(q1, kv1)
    q_in, kv_in, q1, kv1 = together(swap(q1, pair_z), swap(kv1, pair_z1), *held)
    q2, kv2 = join(q1, q_in, kv1, kv_in)
    q_in, kv_in = together(swap(q2, pair_x1), swap(kv2, pair_z2))
    q4, kv4 = join(q2, q_in, kv2, kv_in)
    q_x, kv_y1, kv_y2, *scalars = together(
        swap(q4, pair_x2), swap(kv4, pair_y1), swap(kv4, pair_y2), tiles, bases, rows
    )
    q_core, qx_core, kv_far = swap(q4, pair_core), swap(q_x, pair_core), swap(kv_y1, pair_y2)

    def room(slots):
        return [pltpu.VMEM((slots, 2 * TOK, TOK), narrow), pltpu.VMEM((slots, TOK, TOK), narrow)]

    dq_shape, g_rows = (TOK, 2 * TOK), (2 * TOK, TOK)
    q_all, aux, dq, g = compute(
        first_kernel,
        scalars,
        (q4, q_x, q_core, qx_core, kv4, kv_y1),
        (
            shape(GROUP, QROWS, TOK, dtype=narrow),
            shape(GROUP, 8, 2 * TOK),
            shape(GROUP, *dq_shape),
            shape(HALF, *g_rows),
        ),
        room(8),
        "first",
    )
    dq, far = compute(
        far_kernel,
        scalars,
        (q_all, aux, dq, kv_far),
        (shape(GROUP, *dq_shape), shape(4, *g_rows, dtype=narrow)),
        [pltpu.VMEM((4, *g_rows), wide)] + room(4),
        "far",
    )
    dqa, *others, near = compute(
        last_kernel,
        scalars,
        (q_all, aux, dq, kv_y2),
        (shape(HALF, *dq_shape),) + (shape(2, *dq_shape, dtype=narrow),) * 4 + (shape(4, *g_rows, dtype=narrow),),
        [pltpu.VMEM((GROUP, *dq_shape), wide), pltpu.VMEM((4, *g_rows), wide)] + room(4),
        "last",
    )

    far_in, *others = together(swap(far, pair_y2), *[swap(part, pair_core) for part in others])
    b_in, c_in = jnp.concatenate(others[:2]), jnp.concatenate(others[2:])
    far = g[4:] + far_in.astype(wide)
    near_in, far_in, dq_in = together(
        swap(near, pair_y2), swap(far.astype(narrow), pair_y1), swap((dqa[4:] + c_in.astype(wide)).astype(narrow), pair_x2)
    )
    g, dq = (g[:4] + near_in.astype(wide)) + far_in.astype(wide), (dqa[:4] + b_in.astype(wide)) + dq_in.astype(wide)
    g_in = [swap(g[i : i + 1].astype(narrow), pair) for i, pair in enumerate((pair_z1, pair_z2, pair_z3), 1)]
    dq = dq[:2] + swap(dq[2:].astype(narrow), pair_x1).astype(wide)
    dq_in = swap(dq[1:].astype(narrow), pair_z)
    return pl.pallas_call(
        finish_kernel,
        out_shape=(shape(TOK, 2 * TOK), shape(TOK, TOK), shape(TOK, TOK)),
        in_specs=[spec()] * 6,
        out_specs=(spec(),) * 3,
        compiler_params=params,
        name="finish",
    )(g, *g_in, dq, dq_in)


def solution(mesh):
    rows, cols = P(AXES, None), P(None, AXES)
    return jax.shard_map(
        body,
        mesh=mesh,
        in_specs=(rows, rows, rows, rows, rows, cols, P(), P(), P()),
        out_specs=(rows, rows, rows),
        check_vma=False,
    )
```

```python
import jax
import jax.numpy as jnp
import numpy as np
from jax import lax
from jax.experimental import pallas as pl
from jax.experimental.pallas import tpu as pltpu
from jax.sharding import PartitionSpec as P

AXES = ("qrow", "kcol")
LOG2E = 1.4426950408889634
TOK = 128
AUX = 16
QROWS = 4 * TOK + AUX
GROUP = 16
HALF = GROUP // 2
PARTS = ((0, 8), (12, 16), (8, 12))
LISTS, LIST = 8, GROUP * HALF // 2 + 8
UNROLL = (3, 3, 3)


def coords(i):
    return (i // 64) * 2 + (i // 4) % 2, (i // 16) % 4, (i // 8) % 2, i % 4


def index(z, y, core, x):
    return (((z // 2) * 4 + y) * 2 + core) * 8 + (z % 2) * 4 + x


def pair4(i, flip):
    return 3 - i if flip else i ^ 1


def pair_z(z, y, c, x):
    return 2 * pair4(z // 2, False) + z % 2, y, c, x


def pair_core(z, y, c, x):
    return z, y, 1 - c, x


def pair_z1(z, y, c, x):
    return 2 * pair4(z // 2, True) + z % 2, y, c, x


def pair_z2(z, y, c, x):
    return z ^ 1, y, c, x


def pair_x1(z, y, c, x):
    return z, y, c, pair4(x, c == 1)


def pair_x2(z, y, c, x):
    return z, y, c, pair4(x, c == 0)


def pair_z3(z, y, c, x):
    return pair_z1(*pair_z2(z, y, c, x))


def pair_y1(z, y, c, x):
    return z, pair4(y, c == 1), c, x


def pair_y2(z, y, c, x):
    return z, pair4(y, c == 0), c, x


def partners(pair):
    return np.array([index(*pair(*coords(i))) for i in range(256)])


def joined(pairs):
    table = np.arange(256)[:, None]
    for pair in pairs:
        table = np.concatenate([table, table[partners(pair)]], axis=1)
    return table


def swap(value, pair):
    to = partners(pair)
    return lax.ppermute(value, AXES, [(i, int(to[i])) for i in range(256)])


def slot_tables():
    queries = joined([pair_z, pair_x1, pair_x2, pair_core])
    keys = joined([pair_z1, pair_z2, pair_y1, pair_y2])
    return np.concatenate([queries, keys], axis=1).astype(np.int32)


def prep_kernel(q_ref, g_ref, o_ref, n_ref, k_ref, v_ref, qpay_ref, kvpay_ref):
    rows = [n_ref[0:1, :], n_ref[1:2, :]]
    for head in range(2):
        cols = slice(head * TOK, (head + 1) * TOK)
        qpay_ref[0, head * TOK : (head + 1) * TOK, :] = q_ref[:, cols]
        qpay_ref[0, (2 + head) * TOK : (3 + head) * TOK, :] = g_ref[:, cols]
        product = g_ref[:, cols].astype(jnp.float32) * o_ref[:, cols].astype(jnp.float32)
        rows.append(jnp.sum(product.T, axis=0, keepdims=True))
    exact = jnp.concatenate(rows, axis=0)
    high = exact.astype(jnp.bfloat16).astype(jnp.float32)
    rest = exact - high
    mid = rest.astype(jnp.bfloat16).astype(jnp.float32)
    low = rest - mid
    parts = jnp.concatenate([high, mid, low, jnp.zeros_like(low)], axis=0)
    qpay_ref[0, 4 * TOK :, :] = parts.astype(jnp.bfloat16)
    kvpay_ref[0, 0:TOK, :] = k_ref[...]
    kvpay_ref[0, TOK:, :] = v_ref[...]


def list_kernel(perm_ref, bounds_ref, ids_ref, list_ref, base_ref, rows_ref):
    lane = lax.broadcasted_iota(jnp.int32, (1, TOK), 1)
    for slot in range(GROUP):
        base_ref[slot] = perm_ref[ids_ref[GROUP + slot]] * TOK
        first = perm_ref[ids_ref[slot]] * TOK
        position = first + lane
        start = jnp.zeros((1, TOK), jnp.int32)
        first_start = jnp.int32(0)
        for doc in range(16):
            bound = bounds_ref[doc]
            start = jnp.where(position >= bound, bound, start)
            first_start = jnp.where(first >= bound, bound, first_start)
        base_ref[GROUP + 1 + slot] = first
        base_ref[2 * GROUP + 1 + slot] = first_start
        rows_ref[slot, 0:1, :] = start
        rows_ref[slot, 1:2, :] = position
    base_ref[GROUP] = jnp.int32(-(1 << 20))

    for part, (begin, end) in enumerate(PARTS):
        place = LISTS + part * LIST

        def outer(qs, count):
            first, first_start = base_ref[GROUP + 1 + qs], base_ref[2 * GROUP + 1 + qs]
            held = jnp.int32(GROUP)
            for ks in range(begin, end):
                base = base_ref[ks]
                active = (base <= first) & (first_start <= base + (TOK - 1))
                full = held != GROUP
                entry = qs + 16 * jnp.where(full, held + 32 * ks, ks + 32 * GROUP)
                list_ref[jnp.where(active, place + count, 0)] = entry
                count = count + (active & full).astype(jnp.int32)
                held = jnp.where(active, jnp.where(full, GROUP, ks), held)
            return count + (held != GROUP).astype(jnp.int32)

        count = lax.fori_loop(0, GROUP, outer, jnp.int32(0))
        list_ref[1 + part] = count
        for extra in range(UNROLL[part] - 1):
            list_ref[place + count + extra] = jnp.int32(16 * (GROUP + 32 * GROUP))


def join_kernel(a0, a1, b0, b1, a_ref, b_ref):
    for first, second, ref in ((a0, a1, a_ref), (b0, b1, b_ref)):
        split = first.shape[0]
        ref[0:split] = first[...]
        ref[split:] = second[...]


def hold_kernel(a0, b0, a_ref, b_ref):
    a_ref[...] = a0[...]
    b_ref[...] = b0[...]


def finish_kernel(g_ref, g1, g2, g3, dq_ref, dq_in, query_ref, key_ref, value_ref):
    for ref, rows in ((key_ref, slice(0, TOK)), (value_ref, slice(TOK, 2 * TOK))):
        total = g_ref[0, rows, :]
        for part in (g1, g2, g3):
            total = total + part[0, rows, :].astype(jnp.float32)
        ref[...] = total
    for head in range(2):
        cols = slice(head * TOK, (head + 1) * TOK)
        query_ref[:, cols] = (dq_ref[0, :, cols] + dq_in[0, :, cols].astype(jnp.float32)).T


NT = (((1,), (1,)), ((), ()))


def walk(part, list_ref, base_ref, rows_ref, q_all, aux, kv_refs, kv_all, kt, dq, dkv):
    scale = TOK ** (-0.5)
    begin = PARTS[part][0]
    unroll = UNROLL[part]
    place = LISTS + part * LIST
    sub = lax.broadcasted_iota(jnp.int32, (TOK, TOK), 0)
    for slot in range(PARTS[part][1] - begin):
        block = kv_refs[slot // 4][slot % 4]
        kv_all[slot] = block
        kt[slot] = block[0:TOK, :].T
    dkv[...] = jnp.zeros_like(dkv)

    def tiles(entry):
        qs = entry & (GROUP - 1)
        slots = [(entry >> shift) & 31 for shift in (4, 9)]
        places = [jnp.where(slot == GROUP, 0, slot - begin) for slot in slots]
        bases = [base_ref[slot] for slot in slots]
        q = q_all[qs, 0 : 2 * TOK, :]
        g = q_all[qs, 2 * TOK : 4 * TOK, :]
        k = jnp.concatenate([kv_all[at, 0:TOK, :] for at in places], axis=0)
        v = jnp.concatenate([kv_all[at, TOK:, :] for at in places], axis=0)
        scores = lax.dot_general(k, q, NT, preferred_element_type=jnp.float32)
        dprob = lax.dot_general(v, g, NT, preferred_element_type=jnp.float32)
        start, position = rows_ref[qs, 0:1, :], rows_ref[qs, 1:2, :]
        allowed = [(sub >= start - base) & (sub <= position - base) for base in bases]
        allowed = jnp.concatenate([jnp.concatenate([part, part], axis=1) for part in allowed], axis=0)
        weights = jnp.where(allowed, jnp.exp2(scores * (scale * LOG2E) - aux[qs, 0:1, :]), 0.0)
        dscore = (weights * (dprob - aux[qs, 1:2, :]) * scale).astype(jnp.bfloat16)
        dv = jnp.dot(weights.astype(jnp.bfloat16), g, preferred_element_type=jnp.float32)
        dk = jnp.dot(dscore, q, preferred_element_type=jnp.float32)
        k_t = jnp.concatenate([kt[at] for at in places], axis=1)
        dqt = jnp.dot(k_t, dscore, preferred_element_type=jnp.float32)
        return qs, places, dqt, dk, dv

    def step(i, carry):
        done = [tiles(list_ref[place + unroll * i + j]) for j in range(unroll)]
        for qs, places, dqt, dk, dv in done:
            for at, rows in zip(places, (slice(0, TOK), slice(TOK, 2 * TOK))):
                dkv[at, TOK:, :] += dv[rows]
                dkv[at, 0:TOK, :] += dk[rows]
            dq[qs] += dqt
        return carry

    lax.fori_loop(0, (list_ref[1 + part] + (unroll - 1)) // unroll, step, 0)


def first_kernel(list_ref, base_ref, rows_ref, q0, q1, q2, q3, kv0, kv1, q_all, aux, dq, dkv, kv_all, kt):
    for part, q_ref in enumerate((q0, q1, q2, q3)):
        q_all[4 * part : 4 * part + 4] = q_ref[...]
        for slot in range(4):
            parts = q_ref[slot, 4 * TOK :, :].astype(jnp.float32)
            exact = (parts[8:12] + parts[4:8]) + parts[0:4]
            for head in range(2):
                cols = slice(head * TOK, (head + 1) * TOK)
                aux[4 * part + slot, 0:1, cols] = exact[head : head + 1] * LOG2E
                aux[4 * part + slot, 1:2, cols] = exact[2 + head : 3 + head]
    dq[...] = jnp.zeros_like(dq)
    walk(0, list_ref, base_ref, rows_ref, q_all, aux, (kv0, kv1), kv_all, kt, dq, dkv)


def far_kernel(list_ref, base_ref, rows_ref, q_all, aux, before, kv_ref, dq, out_ref, dkv, kv_all, kt):
    dq[...] = before[...]
    walk(1, list_ref, base_ref, rows_ref, q_all, aux, (kv_ref,), kv_all, kt, dq, dkv)
    out_ref[...] = dkv[...].astype(jnp.bfloat16)


def last_kernel(list_ref, base_ref, rows_ref, q_all, aux, before, kv_ref, dqa_ref, *refs):
    outs, (out_ref, dq, dkv, kv_all, kt) = refs[:4], refs[4:]
    dq[...] = before[...]
    walk(2, list_ref, base_ref, rows_ref, q_all, aux, (kv_ref,), kv_all, kt, dq, dkv)
    dqa_ref[...] = dq[0:HALF]
    for i, ref in enumerate(outs):
        ref[...] = dq[HALF + 2 * i : HALF + 2 * i + 2].astype(jnp.bfloat16)
    out_ref[...] = dkv[...].astype(jnp.bfloat16)


def spec(space=pltpu.VMEM):
    return pl.BlockSpec(memory_space=space)


def together(*arrays):
    return lax.optimization_barrier(arrays)


def whole(array):
    return pl.BlockSpec(array.shape, lambda i: (0, 0))


def body(queries, keys, values, out_grad, outputs, log_norm, perm_blocks, doc_bounds, block_map):
    del block_map
    me = lax.axis_index("qrow") * lax.axis_size("kcol") + lax.axis_index("kcol")
    ids = jnp.asarray(slot_tables())[me]
    params = pltpu.CompilerParams(vmem_limit_bytes=40 * 1024 * 1024)
    q1, kv1 = pl.pallas_call(
        prep_kernel,
        out_shape=(
            jax.ShapeDtypeStruct((1, QROWS, TOK), jnp.bfloat16),
            jax.ShapeDtypeStruct((1, 2 * TOK, TOK), jnp.bfloat16),
        ),
        grid=(1,),
        in_specs=[whole(a) for a in (queries, out_grad, outputs, log_norm, keys, values)],
        out_specs=(spec(), spec()),
        compiler_params=pltpu.CompilerParams(vmem_limit_bytes=60 * 1024 * 1024),
        name="prep",
    )(queries, out_grad, outputs, log_norm, keys, values)
    tiles, bases, rows = pl.pallas_call(
        list_kernel,
        out_shape=(
            jax.ShapeDtypeStruct((LISTS + 3 * LIST,), jnp.int32),
            jax.ShapeDtypeStruct((64,), jnp.int32),
            jax.ShapeDtypeStruct((GROUP, 8, TOK), jnp.int32),
        ),
        in_specs=[spec(pltpu.SMEM)] * 3,
        out_specs=(spec(pltpu.SMEM), spec(pltpu.SMEM), spec()),
        compiler_params=params,
        name="tiles",
    )(perm_blocks, doc_bounds, ids)

    narrow, wide = jnp.bfloat16, jnp.float32

    def shape(*dims, dtype=wide):
        return jax.ShapeDtypeStruct(dims, dtype)

    def join(q0, q_in, kv0, kv_in):
        n = 2 * q0.shape[0]
        return pl.pallas_call(
            join_kernel,
            out_shape=(shape(n, *q0.shape[1:], dtype=narrow), shape(n, *kv0.shape[1:], dtype=narrow)),
            in_specs=[spec()] * 4,
            out_specs=(spec(),) * 2,
            compiler_params=params,
            name="join",
        )(q0, q_in, kv0, kv_in)

    def compute(kernel, scalars, arrays, outs, scratch, name):
        return pl.pallas_call(
            kernel,
            out_shape=outs,
            in_specs=[spec(pltpu.SMEM)] * 2 + [spec()] * (1 + len(arrays)),
            out_specs=(spec(),) * len(outs),
            scratch_shapes=scratch,
            compiler_params=params,
            cost_estimate=pl.CostEstimate(flops=3 * 10**9, bytes_accessed=10**7, transcendentals=10**6),
            name=name,
        )(*scalars, *arrays)

    held = pl.pallas_call(
        hold_kernel,
        out_shape=(shape(*q1.shape, dtype=narrow), shape(*kv1.shape, dtype=narrow)),
        in_specs=[spec()] * 2,
        out_specs=(spec(),) * 2,
        compiler_params=params,
        name="hold",
    )(q1, kv1)
    q_in, kv_in, q1, kv1 = together(swap(q1, pair_z), swap(kv1, pair_z1), *held)
    q2, kv2 = join(q1, q_in, kv1, kv_in)
    q_in, kv_in = together(swap(q2, pair_x1), swap(kv2, pair_z2))
    q4, kv4 = join(q2, q_in, kv2, kv_in)
    q_x, kv_y1, kv_y2, *scalars = together(
        swap(q4, pair_x2), swap(kv4, pair_y1), swap(kv4, pair_y2), tiles, bases, rows
    )
    q_core, qx_core, kv_far = swap(q4, pair_core), swap(q_x, pair_core), swap(kv_y1, pair_y2)

    def room(slots):
        return [pltpu.VMEM((slots, 2 * TOK, TOK), narrow), pltpu.VMEM((slots, TOK, TOK), narrow)]

    dq_shape, g_rows = (TOK, 2 * TOK), (2 * TOK, TOK)
    q_all, aux, dq, g = compute(
        first_kernel,
        scalars,
        (q4, q_x, q_core, qx_core, kv4, kv_y1),
        (
            shape(GROUP, QROWS, TOK, dtype=narrow),
            shape(GROUP, 8, 2 * TOK),
            shape(GROUP, *dq_shape),
            shape(HALF, *g_rows),
        ),
        room(8),
        "first",
    )
    dq, far = compute(
        far_kernel,
        scalars,
        (q_all, aux, dq, kv_far),
        (shape(GROUP, *dq_shape), shape(4, *g_rows, dtype=narrow)),
        [pltpu.VMEM((4, *g_rows), wide)] + room(4),
        "far",
    )
    dqa, *others, near = compute(
        last_kernel,
        scalars,
        (q_all, aux, dq, kv_y2),
        (shape(HALF, *dq_shape),) + (shape(2, *dq_shape, dtype=narrow),) * 4 + (shape(4, *g_rows, dtype=narrow),),
        [pltpu.VMEM((GROUP, *dq_shape), wide), pltpu.VMEM((4, *g_rows), wide)] + room(4),
        "last",
    )

    far_in, *others = together(swap(far, pair_y2), *[swap(part, pair_core) for part in others])
    b_in, c_in = jnp.concatenate(others[:2]), jnp.concatenate(others[2:])
    far = g[4:] + far_in.astype(wide)
    near_in, far_in, dq_in = together(
        swap(near, pair_y2), swap(far.astype(narrow), pair_y1), swap((dqa[4:] + c_in.astype(wide)).astype(narrow), pair_x2)
    )
    g, dq = (g[:4] + near_in.astype(wide)) + far_in.astype(wide), (dqa[:4] + b_in.astype(wide)) + dq_in.astype(wide)
    g_in = [swap(g[i : i + 1].astype(narrow), pair) for i, pair in enumerate((pair_z1, pair_z2, pair_z3), 1)]
    dq = dq[:2] + swap(dq[2:].astype(narrow), pair_x1).astype(wide)
    dq_in = swap(dq[1:].astype(narrow), pair_z)
    return pl.pallas_call(
        finish_kernel,
        out_shape=(shape(TOK, 2 * TOK), shape(TOK, TOK), shape(TOK, TOK)),
        in_specs=[spec()] * 6,
        out_specs=(spec(),) * 3,
        compiler_params=params,
        name="finish",
    )(g, *g_in, dq, dq_in)


def solution(mesh):
    rows, cols = P(AXES, None), P(None, AXES)
    return jax.shard_map(
        body,
        mesh=mesh,
        in_specs=(rows, rows, rows, rows, rows, cols, P(), P(), P()),
        out_specs=(rows, rows, rows),
        check_vma=False,
    )
```
